32 devices in a mesh: row: 8 (over z, x), col: 4 (over y, core).
Axes of the slice: x: 2, y: 2, z: 4, core: 2. Of those that a mesh axis runs over, the one named last changes fastest.
Arguments:
- a_blocks: float32 [8, 4, 8, 128, 128], P('row', 'col'), may hold values from -6 to 6
- a_coords: int32 [8, 4, 2, 8], P('row', 'col'), may hold values from 0 to 63, as said below
- b_blocks: float32 [8, 4, 32, 128, 128], P('row', 'col'), may hold values from -0.5 to 0.5
- b_coords: int32 [8, 4, 2, 32], P('row', 'col'), may hold values from 0 to 31, as said below
Outputs:
- product: float32 [2048, 8192], P('row', 'col')
The draws below stay inside these ranges and needn't reach their ends.
Inputs may be any that keep to these rules, and one draw needn't show every extreme that they name: `a_coords`: each tile lists 8 distinct block positions, exactly 4 of them in each of its 2 column pieces of 32 block columns, with distinct block columns inside one piece; entry 0 is a block row below 2, entry 1 a block column below 64. `b_coords`: each tile lists 32 distinct block positions; entry 0 is a block row below 32, entry 1 a block column below 16.
All inputs are finite; a program needn't handle non-finite values.
Results may differ from the reference program's by a relative error of at most 0.0003.
Values sent between devices are 32-bit elements; how exact they have to be, the bound alone decides.
No kernel may reach another device: no remote copies, remote signals or barrier semaphores. Data moves between devices by JAX's collectives and lax.ppermute only.
A program may use at most 64 MiB of HBM per device.

```python
import jax
import jax.numpy as jnp
from jax import lax

BS = 128
KB = 32
RB = 2
CB = 16
STEPS = 2
GROWS = 8
GCOLS = 4
KPC = 2
NA = 8
NB = 32
MROWS = 2048
MCOLS = 8192


def draw_a_coords(key, part):
    keys = jax.random.split(jax.random.fold_in(key, 11), GROWS * GCOLS)
    per_piece = NA // KPC

    def one_tile(tile_key):
        first, second = jax.random.split(tile_key)
        piece_keys = jax.random.split(first, KPC)

        def one_piece(piece_key, piece):
            col_key, row_key = jax.random.split(piece_key)
            columns = jax.random.permutation(col_key, KB)[:per_piece]
            rows = jax.random.randint(row_key, (per_piece,), 0, RB)
            return jnp.stack([rows, columns + piece * KB])
        pieces = jax.vmap(one_piece)(piece_keys, jnp.arange(KPC, dtype=jnp.int32))
        joined = jnp.transpose(pieces, (1, 0, 2)).reshape(2, NA)
        order = jax.random.permutation(second, NA)
        return joined[:, order]
    return jax.vmap(one_tile)(keys).reshape(GROWS, GCOLS, 2, NA).astype(jnp.int32)


def draw_b_coords(key, part):
    a_pos_all = draw_a_coords(key, part)
    keys = jax.random.split(jax.random.fold_in(key, 23), GROWS * GCOLS)
    per_piece = NA // KPC

    def one_tile(tile_key):
        chosen = jax.random.permutation(tile_key, KB * CB)[:NB]
        return jnp.stack([chosen // CB, chosen % CB])
    base = jax.vmap(one_tile)(keys).reshape(GROWS, GCOLS, 2, NB).astype(jnp.int32)
    pick_key = jax.random.fold_in(key, 37)
    row_key, step_key, fill_key = jax.random.split(pick_key, 3)
    rows_pick = jax.random.randint(row_key, (GCOLS,), 0, GROWS).astype(jnp.int32)
    steps_pick = jax.random.randint(step_key, (GCOLS,), 0, STEPS).astype(jnp.int32)
    fill_keys = jax.random.split(fill_key, GCOLS)
    columns_all = jnp.arange(GCOLS, dtype=jnp.int32)

    def worst_tile(grid_col, piece_row, step, tile_key):
        user_row = ((piece_row - step) % GROWS).astype(jnp.int32)
        owner = (piece_row // KPC).astype(jnp.int32)
        piece = (piece_row % KPC).astype(jnp.int32)
        a_pos = a_pos_all[user_row, owner]
        outside = (a_pos[1] // KB != piece).astype(jnp.int32)
        score = outside * NA + jnp.arange(NA, dtype=jnp.int32)
        order = jnp.argsort(score, stable=True)
        kcols = (a_pos[1][order[:per_piece]] % KB).astype(jnp.int32)
        chosen = jax.random.permutation(tile_key, per_piece * CB)[:NB]
        return jnp.stack([kcols[chosen // CB], chosen % CB]).astype(jnp.int32)
    worst = jax.vmap(worst_tile)(columns_all, rows_pick, steps_pick, fill_keys)
    base = base.at[rows_pick, columns_all].set(worst)
    return base.astype(jnp.int32)


def level_of(own_key, dims, cuts, least, top_value):
    def one(axis_at, shards_of):
        draws = jax.random.uniform(jax.random.fold_in(jax.random.fold_in(own_key, 6), axis_at), (shards_of,), jnp.float32, least / len(cuts), top_value / len(cuts))
        return jnp.repeat(jnp.exp(draws), dims[axis_at] // shards_of).reshape((-1,) + (1,) * (len(dims) - axis_at - 1))

    loudness = one(*cuts[0])
    for cut in cuts[1:]:
        loudness = loudness * one(*cut)
    return loudness


def gaussian(stream_key, dims, spread, reach, cuts=(), kind=jnp.bfloat16):
    level = level_of(stream_key, dims, cuts, -0.22, 0.18) if cuts else 1.0
    entries = jax.random.normal(stream_key, dims, jnp.float32) * spread * level
    return jnp.minimum(jnp.maximum(entries, -reach), reach).astype(kind)


def setup_inputs(seed: int = 0) -> dict:
    splits = jax.random.split(jax.random.key(seed), 5)
    a_blocks = gaussian(splits[0], (GROWS, GCOLS, NA, BS, BS), 1.0, 6.0, ((0, 8), (1, 4)), jnp.float32)
    a_coords = draw_a_coords(jax.random.fold_in(splits[4], 71), 0)
    b_blocks = gaussian(splits[2], (GROWS, GCOLS, NB, BS, BS), BS ** -0.5, 0.5, ((0, 8), (1, 4)), jnp.float32)
    b_coords = draw_b_coords(jax.random.fold_in(splits[4], 71), 0)
    return dict(a_blocks=a_blocks, a_coords=a_coords, b_blocks=b_blocks, b_coords=b_coords)


def tile_product(a_blk, a_pos, b_blk, b_pos, piece):
    high = lax.Precision.HIGHEST
    in_piece = (a_pos[1] // KB) == piece
    kcol = a_pos[1] % KB
    match = ((kcol[:, None] == b_pos[0][None, :]) & in_piece[:, None]).astype(jnp.float32)
    rowsel = (a_pos[0][None, :] == jnp.arange(RB, dtype=jnp.int32)[:, None]).astype(jnp.float32)
    coef = rowsel[:, None, :] * jnp.transpose(match)[None, :, :]
    wide = jnp.einsum("rbm,mxy->rbxy", coef, a_blk, precision=high)
    prods = jnp.einsum("rbxy,byz->rbxz", wide, b_blk, precision=high)
    colsel = (b_pos[1][None, :] == jnp.arange(CB, dtype=jnp.int32)[:, None]).astype(jnp.float32)
    out = jnp.einsum("cb,rbxz->rxcz", colsel, prods, precision=high)
    return out.reshape(RB * BS, CB * BS)


def reference(a_blocks, a_coords, b_blocks, b_coords):
    def one_tile(flat):
        row_idx = (flat // GCOLS).astype(jnp.int32)
        col_idx = (flat % GCOLS).astype(jnp.int32)
        total = jnp.zeros((RB * BS, CB * BS), jnp.float32)
        for step in range(STEPS):
            piece_row = ((row_idx + step) % GROWS).astype(jnp.int32)
            owner = (piece_row // KPC).astype(jnp.int32)
            half = (piece_row % KPC).astype(jnp.int32)
            total = total + tile_product(a_blocks[row_idx, owner], a_coords[row_idx, owner],
                                         b_blocks[piece_row, col_idx], b_coords[piece_row, col_idx], half)
        return total

    tiles = lax.map(one_tile, jnp.arange(GROWS * GCOLS, dtype=jnp.int32))
    tiles = tiles.reshape(GROWS, GCOLS, RB * BS, CB * BS)
    return jnp.transpose(tiles, (0, 2, 1, 3)).reshape(MROWS, MCOLS)
```

```python
import functools

import jax
import jax.numpy as jnp
from jax import lax
from jax.experimental import pallas as pl
from jax.experimental.pallas import tpu as pltpu
from jax.sharding import PartitionSpec as P

KB = 32
RB = 2
CB = 16
STEPS = 2
CHUNKS = (32,)
NOTE = 8

VMEM = pl.BlockSpec(memory_space=pltpu.VMEM)
SMEM = pl.BlockSpec(memory_space=pltpu.SMEM)


def pack_kernel(count, halves_ref, pos_ref, a_ref, *out_refs):
    stored, edge = a_ref.shape[0], a_ref.shape[1]
    lane = lax.broadcasted_iota(jnp.int32, (NOTE, edge), 1)
    line = lax.broadcasted_iota(jnp.int32, (NOTE, edge), 0)
    for s, out in enumerate(out_refs):
        half = halves_ref[s]
        place = jnp.int32(0)
        note = jnp.zeros((NOTE, edge), jnp.int32)
        for m in range(stored):
            row, col = pos_ref[0, m], pos_ref[1, m]
            mine = (col // KB == half) & (place < count)
            at = place

            @pl.when(mine)
            def _():
                out[pl.ds(pl.multiple_of(at * edge, edge), edge), :] = a_ref[m]

            hit = mine & (lane == at)
            note = jnp.where(hit & (line == 0), row, note)
            note = jnp.where(hit & (line == 1), col % KB, note)
            place = place + mine.astype(jnp.int32)
        out[pl.ds(count * edge, NOTE), :] = note.astype(jnp.float32)


def pack(halves, pos, blocks, count):
    edge = blocks.shape[1]
    shape = jax.ShapeDtypeStruct((count * edge + NOTE, edge), jnp.float32)
    return pl.pallas_call(
        functools.partial(pack_kernel, count),
        out_shape=(shape,) * STEPS,
        in_specs=[SMEM, SMEM, VMEM],
        out_specs=(VMEM,) * STEPS,
        compiler_params=pltpu.CompilerParams(vmem_limit_bytes=16 << 20),
        cost_estimate=pl.CostEstimate(flops=0, bytes_accessed=4 * blocks.size * 4, transcendentals=0),
    )(halves, pos, blocks)


def split(x):
    high = x.astype(jnp.bfloat16)
    return high, (x - high.astype(jnp.float32)).astype(jnp.bfloat16)


def dot3(a, b):
    ah, al = split(a)
    bh, bl = split(b)
    dot = functools.partial(jnp.dot, preferred_element_type=jnp.float32)
    return dot(ah, bh) + (dot(ah, bl) + dot(al, bh))


def add_kernel(count, first, has_total, a_pos_ref, b_pos_ref, a_ref, b_ref, *refs):
    out_ref, lut = refs[-2], refs[-1]
    edge = b_ref.shape[1]
    if has_total:
        out_ref[...] = refs[0][...]
    else:
        out_ref[...] = jnp.zeros_like(out_ref)

    @pl.loop(0, KB)
    def _(k):
        lut[k] = -1

    for m in range(count):
        lut[a_pos_ref[1, m]] = m

    @pl.loop(0, b_ref.shape[0])
    def _(m):
        which = lut[b_pos_ref[0, first + m]]

        @pl.when(which >= 0)
        def _():
            row = pl.multiple_of(a_pos_ref[0, which] * edge, edge)
            col = pl.multiple_of(b_pos_ref[1, first + m] * edge, edge)
            at = pl.multiple_of(which * edge, edge)
            part = dot3(a_ref[pl.ds(at, edge), :], b_ref[m])
            out_ref[pl.ds(row, edge), pl.ds(col, edge)] += part


def add_products(piece, piece_pos, b, b_pos, first, total):
    edge = b.shape[1]
    count = piece_pos.shape[1]
    shape = jax.ShapeDtypeStruct((RB * edge, CB * edge), jnp.float32)
    extra = () if total is None else (total,)
    return pl.pallas_call(
        functools.partial(add_kernel, count, first, total is not None),
        out_shape=shape,
        in_specs=[SMEM, SMEM, VMEM, VMEM] + [VMEM] * len(extra),
        out_specs=VMEM,
        scratch_shapes=[pltpu.SMEM((KB,), jnp.int32)],
        compiler_params=pltpu.CompilerParams(vmem_limit_bytes=24 << 20),
        cost_estimate=pl.CostEstimate(
            flops=6 * b.size * edge, bytes_accessed=4 * (b.size + 2 * shape.size), transcendentals=0
        ),
    )(piece_pos, b_pos, piece, b, *extra)


def per_device(a_blocks, a_coords, b_blocks, b_coords):
    rows, cols = lax.axis_size("row"), lax.axis_size("col")
    per_col = rows // cols
    my_row, my_col = lax.axis_index("row"), lax.axis_index("col")
    a, a_pos, b, b_pos = a_blocks[0, 0], a_coords[0, 0], b_blocks[0, 0], b_coords[0, 0]
    count = a.shape[0] // per_col
    edge = a.shape[1]

    back = [((r + 1) % rows, r) for r in range(rows)]
    ring = functools.partial(lax.ppermute, axis_name="row", perm=back)
    starts = [sum(CHUNKS[:k]) for k in range(len(CHUNKS))]
    next_b = [ring(b[s : s + n]) for s, n in zip(starts, CHUNKS, strict=True)]
    next_pos = ring(b_pos)

    halves = jnp.stack([(my_row + s) % rows % per_col for s in range(STEPS)]).astype(jnp.int32)
    packed = pack(halves, a_pos, a, count)
    pieces, piece_pos = [], []
    for s in range(STEPS):
        owner = (my_row + s) % rows // per_col
        got = jnp.where(my_col == owner, packed[s], 0.0)
        for d in range(1, cols):
            pairs = []
            for r in range(rows):
                o = (r + s) % rows // per_col
                pairs.append((r * cols + o, r * cols + (o + d) % cols))
            got = got + lax.ppermute(packed[s], ("row", "col"), pairs)
        pieces.append(got)
        piece_pos.append(got[count * edge : count * edge + 2, :count].astype(jnp.int32))

    total = add_products(pieces[0], piece_pos[0], b, b_pos, 0, None)
    for s, got_b in zip(starts, next_b, strict=True):
        total = add_products(pieces[1], piece_pos[1], got_b, next_pos, s, total)
    return total


def solution(mesh):
    return jax.shard_map(
        per_device,
        mesh=mesh,
        in_specs=(
            P("row", "col", None, None, None),
            P("row", "col", None, None),
            P("row", "col", None, None, None),
            P("row", "col", None, None),
        ),
        out_specs=P("row", "col"),
        check_vma=False,
    )
```

```python
import functools

import jax
import jax.numpy as jnp
from jax import lax
from jax.experimental import pallas as pl
from jax.experimental.pallas import tpu as pltpu
from jax.sharding import PartitionSpec as P

KB = 32
RB = 2
CB = 16
STEPS = 2
FIRST = 8
KEEP = 6
MORE = 4
GRANT = 56 << 20
NOTE = 8

VMEM = pl.BlockSpec(memory_space=pltpu.VMEM)
SMEM = pl.BlockSpec(memory_space=pltpu.SMEM)
ANY = pl.BlockSpec(memory_space=pl.ANY)


def cost(flops, size):
    return pl.CostEstimate(flops=flops, bytes_accessed=4 * size, transcendentals=0)


def pack_kernel(count, pieces, pos_ref, a_ref, out_ref, sem):
    stored, edge = a_ref.shape[0], a_ref.shape[1]
    span = count * edge + NOTE
    lane = lax.broadcasted_iota(jnp.int32, (NOTE, edge), 1)
    line = lax.broadcasted_iota(jnp.int32, (NOTE, edge), 0)
    notes = [jnp.zeros((NOTE, edge), jnp.int32) for _ in range(pieces)]
    places = [jnp.int32(0) for _ in range(pieces)]
    for m in range(stored):
        row, col = pos_ref[0, m], pos_ref[1, m]
        piece = col // KB
        at = places[-1]
        for h in range(pieces - 1):
            at = jnp.where(piece == h, places[h], at)
        start = pl.multiple_of(piece * span + at * edge, 8)
        pltpu.make_async_copy(a_ref.at[m], out_ref.at[pl.ds(start, edge)], sem).start()
        for h in range(pieces):
            mine = piece == h
            hit = mine & (lane == at)
            notes[h] = jnp.where(hit & (line == 0), row, notes[h])
            notes[h] = jnp.where(hit & (line == 1), col % KB, notes[h])
            places[h] = places[h] + mine.astype(jnp.int32)
    for h in range(pieces):
        out_ref[pl.ds(h * span + count * edge, NOTE), :] = notes[h].astype(jnp.float32)
    for m in range(stored):
        pltpu.make_async_copy(a_ref.at[m], out_ref.at[pl.ds(m * edge, edge)], sem).wait()


def pack(pos, blocks, count):
    stored, edge = blocks.shape[:2]
    pieces = stored // count
    return pl.pallas_call(
        functools.partial(pack_kernel, count, pieces),
        out_shape=jax.ShapeDtypeStruct((pieces * (count * edge + NOTE), edge), jnp.float32),
        in_specs=[SMEM, ANY],
        out_specs=VMEM,
        scratch_shapes=[pltpu.SemaphoreType.DMA],
        compiler_params=pltpu.CompilerParams(vmem_limit_bytes=8 << 20),
        cost_estimate=cost(0, 2 * blocks.size),
    )(pos, blocks)


def select_kernel(sizes, half_ref, a_pos_ref, b_pos_ref, b_ref, *refs):
    outs, (lut, index, sem) = refs[: len(sizes)], refs[len(sizes) :]
    for k in range(KB):
        lut[k] = 0
    for m in range(a_pos_ref.shape[1]):

        @pl.when(a_pos_ref[1, m] // KB == half_ref[0])
        def _():
            lut[a_pos_ref[1, m] % KB] = 1

    n = jnp.int32(0)
    for m in range(FIRST, b_ref.shape[0]):
        index[n] = m
        n = n + lut[b_pos_ref[0, m]]

    def each(act):
        start = 0
        for size, out in zip(sizes, outs, strict=True):

            @pl.loop(start, jnp.minimum(n, start + size))
            def _(k):
                act(pltpu.make_async_copy(b_ref.at[index[k]], out.at[k - start], sem))

            start += size

    each(lambda copy: copy.start())
    each(lambda copy: copy.wait())


def select(half, a_pos, b_pos, b, sizes):
    return pl.pallas_call(
        functools.partial(select_kernel, sizes),
        out_shape=tuple(jax.ShapeDtypeStruct((n,) + b.shape[1:], b.dtype) for n in sizes),
        in_specs=[SMEM, SMEM, SMEM, ANY],
        out_specs=(VMEM,) * len(sizes),
        scratch_shapes=[
            pltpu.SMEM((KB,), jnp.int32),
            pltpu.SMEM((b.shape[0] + 1,), jnp.int32),
            pltpu.SemaphoreType.DMA,
        ],
        compiler_params=pltpu.CompilerParams(vmem_limit_bytes=GRANT),
        cost_estimate=cost(0, b.size),
    )(half, a_pos, b_pos, b)


def split(x):
    high = x.astype(jnp.bfloat16)
    return high, (x - high.astype(jnp.float32)).astype(jnp.bfloat16)


def product(a_wide, b):
    high, low = split(b)
    wide = jnp.concatenate(
        [jnp.concatenate([high, low], axis=1), jnp.concatenate([high, jnp.zeros_like(low)], axis=1)], axis=0
    )
    both = jnp.dot(a_wide, wide, preferred_element_type=jnp.float32)
    edge = b.shape[1]
    return both[:, :edge] + both[:, edge:]


def listed(lut, lists, a_pos_ref, b_pos_ref, first, stop):
    for k in range(KB):
        lut[k] = -1
    for m in range(a_pos_ref.shape[1]):
        lut[a_pos_ref[1, m]] = m
    n = jnp.int32(0)
    for m in range(first, stop):
        which = lut[b_pos_ref[0, m]]
        lists[0, n] = which
        lists[1, n] = a_pos_ref[0, jnp.maximum(which, 0)]
        lists[2, n] = b_pos_ref[1, m]
        lists[3, n] = m
        n = n + (which >= 0).astype(jnp.int32)
    return n


def add_listed(lists, low, high, a_wide, b_block, out_ref):
    edge = a_wide.shape[1]

    def one(n):
        return product(a_wide[lists[0, n]], b_block(n))

    def put(n, part):
        row = pl.multiple_of(lists[1, n] * edge, edge)
        col = pl.multiple_of(lists[2, n] * edge, edge)
        out_ref[pl.ds(row, edge), pl.ds(col, edge)] += part

    pairs = jnp.maximum(high - low, 0) // 2

    @pl.loop(0, pairs)
    def _(t):
        n = low + 2 * t
        parts = one(n), one(n + 1)
        put(n, parts[0])
        put(n + 1, parts[1])

    @pl.when(low + 2 * pairs < high)
    def _():
        put(high - 1, one(high - 1))


def widen(a_wide, x):
    count, edge = a_wide.shape[:2]
    for m in range(count):
        high, low = split(x[pl.ds(m * edge, edge), :])
        a_wide[m, :, :edge] = high
        a_wide[m, :, edge:] = low


def spot(ref, edge, row, col):
    rows = pl.ds(pl.multiple_of(row * edge, edge), edge)
    return ref.at[rows, pl.ds(pl.multiple_of(col * edge, edge), edge)]


def level(n):
    return (n > KEEP).astype(jnp.int32) + (n > KEEP + MORE).astype(jnp.int32)


def early_kernel(*refs):
    (first_ref, next_pos_ref, asked_ref, use_ref, pos0_ref, pos1_ref, b_pos_ref), refs = refs[:7], refs[7:]
    mine_ref, other_ref, b_ref, out_ref, wide_out, plan, code_ref, *refs = refs
    acc, nought, x0, x1, b_v, first_v, wide0, wide1, lut, lists, firsts, seen, sems = refs
    sem, wide_copy = sems.at[0], pltpu.make_async_copy(wide1, wide_out, sems.at[1])
    count, edge = wide0.shape[:2]
    tile = b_pos_ref.shape[1]
    span = count * edge + NOTE

    def load(s, src, x):
        start = pl.multiple_of(use_ref[2 * s] * span, 8)
        return pltpu.make_async_copy(src.at[pl.ds(start, count * edge)], x, sems.at[2 + s])

    for s, x in enumerate((x0, x1)):
        for src, on in ((mine_ref, 1), (other_ref, 0)):

            @pl.when(use_ref[2 * s + 1] == on)
            def _():
                load(s, src, x).start()

    def block(k):
        return pltpu.make_async_copy(b_ref.at[lists[3, k]], b_v.at[k], sems.at[4])

    def early_block(k):
        start = pl.multiple_of(firsts[3, k] * edge, edge)
        return pltpu.make_async_copy(first_ref.at[pl.ds(start, edge)], first_v.at[k], sems.at[5])

    n = listed(lut, lists, pos0_ref, b_pos_ref, 0, tile)
    pl.loop(0, n)(lambda k: block(k).start())
    n1 = listed(lut, firsts, pos1_ref, next_pos_ref, 0, FIRST)
    pl.loop(0, n1)(lambda k: early_block(k).start())
    for k in range(RB * CB):
        seen[k] = 0
    nought[...] = jnp.zeros_like(nought)

    def touch(list_ref):
        def act(k):
            row, col = list_ref[1, k], list_ref[2, k]
            seen[row * CB + col] = 1
            spot(acc, edge, row, col)[...] = nought[...]

        return act

    pl.loop(0, n)(touch(lists))
    pl.loop(0, n1)(touch(firsts))
    for row in range(RB):
        for col in range(CB):

            @pl.when(seen[row * CB + col] == 0)
            def _():
                pltpu.make_async_copy(nought, spot(out_ref, edge, row, col), sem).start()

    load(1, mine_ref, x1).wait()
    widen(wide1, x1)
    wide_copy.start()
    load(0, mine_ref, x0).wait()
    widen(wide0, x0)
    pl.loop(0, n)(lambda k: block(k).wait())
    add_listed(lists, 0, n, wide0, lambda k: b_v[k], acc)
    pl.loop(0, n1)(lambda k: early_block(k).wait())
    add_listed(firsts, 0, n1, wide1, lambda k: first_v[k], acc)
    for row in range(RB):
        for col in range(CB):

            @pl.when(seen[row * CB + col] == 1)
            def _():
                pltpu.make_async_copy(spot(acc, edge, row, col), spot(out_ref, edge, row, col), sem).start()

    gets = listed(lut, plan, pos1_ref, next_pos_ref, FIRST, tile)
    plan[0, tile] = gets
    for k in range(KB):
        lut[k] = 0
    for m in range(asked_ref.shape[1]):

        @pl.when(asked_ref[1, m] // KB == use_ref[2 * STEPS + 1])
        def _():
            lut[asked_ref[1, m] % KB] = 1

    gives = jnp.int32(0)
    for m in range(FIRST, tile):
        gives = gives + lut[b_pos_ref[0, m]]
    even = use_ref[2 * STEPS] == 0
    code_ref[0] = level(jnp.where(even, gets, gives)) + 4 * level(jnp.where(even, gives, gets))
    pltpu.make_async_copy(acc, out_ref, sem).wait()
    wide_copy.wait()


def early(first_b, coords, mine, other, b):
    tile, edge = b.shape[:2]
    count = coords[3].shape[1]
    wide = (count, edge, 2 * edge)
    total = (RB * edge, CB * edge)
    return pl.pallas_call(
        early_kernel,
        out_shape=(
            jax.ShapeDtypeStruct(total, jnp.float32),
            jax.ShapeDtypeStruct(wide, jnp.bfloat16),
            jax.ShapeDtypeStruct((4, tile + 1), jnp.int32),
            jax.ShapeDtypeStruct((1,), jnp.int32),
        ),
        in_specs=[ANY] + [SMEM] * len(coords) + [ANY] * 3,
        out_specs=(ANY, ANY, SMEM, SMEM),
        scratch_shapes=[
            pltpu.VMEM(total, jnp.float32),
            pltpu.VMEM((edge, edge), jnp.float32),
            pltpu.VMEM((count * edge, edge), jnp.float32),
            pltpu.VMEM((count * edge, edge), jnp.float32),
            pltpu.VMEM(b.shape, jnp.float32),
            pltpu.VMEM((FIRST, edge, edge), jnp.float32),
            pltpu.VMEM(wide, jnp.bfloat16),
            pltpu.VMEM(wide, jnp.bfloat16),
            pltpu.SMEM((KB,), jnp.int32),
            pltpu.SMEM((4, tile + 1), jnp.int32),
            pltpu.SMEM((4, tile + 1), jnp.int32),
            pltpu.SMEM((RB * CB,), jnp.int32),
            pltpu.SemaphoreType.DMA((6,)),
        ],
        compiler_params=pltpu.CompilerParams(vmem_limit_bytes=GRANT),
        cost_estimate=cost(6 * b.size * edge, 2 * b.size),
    )(first_b, *coords, mine, other, b)


def empty(shapes):
    return pl.pallas_call(
        lambda *refs: None,
        out_shape=tuple(jax.ShapeDtypeStruct(x, jnp.float32) for x in shapes),
        out_specs=(ANY,) * len(shapes),
    )()


def late_kernel(side_ref, plan, wide_ref, kept_ref, total_ref, *refs):
    sides, (out_ref, acc, wide, got, seen, sems) = refs[:4], refs[4:]
    edge = wide.shape[1]
    tile = plan.shape[1] - 1
    n = plan[0, tile]

    def load(row, col):
        return pltpu.make_async_copy(spot(out_ref, edge, row, col), spot(acc, edge, row, col), sems.at[2])

    def store(row, col):
        return pltpu.make_async_copy(spot(acc, edge, row, col), spot(out_ref, edge, row, col), sems.at[3])

    def touched(act):
        for row in range(RB):
            for col in range(CB):

                @pl.when(seen[row * CB + col] == 1)
                def _():
                    act(row, col)

    @pl.when(n > 0)
    def _():
        def fetch(act):
            getattr(pltpu.make_async_copy(wide_ref, wide, sems.at[4]), act)()
            getattr(pltpu.make_async_copy(kept_ref, got.at[pl.ds(0, KEEP)], sems.at[0]), act)()

        def fetch_more(act):
            for side in range(2):
                for k, (start, least) in enumerate(((KEEP, KEEP), (KEEP + MORE, KEEP + MORE))):
                    src = sides[2 * side + k]

                    @pl.when((side_ref[0] == side) & (n > least))
                    def _():
                        getattr(pltpu.make_async_copy(src, got.at[pl.ds(start, src.shape[0])], sems.at[1]), act)()

        fetch("start")
        for k in range(RB * CB):
            seen[k] = 0

        @pl.loop(0, n)
        def _(k):
            row, col = plan[1, k], plan[2, k]

            @pl.when(seen[row * CB + col] == 0)
            def _():
                seen[row * CB + col] = 1
                load(row, col).start()

        fetch_more("start")
        fetch("wait")
        touched(lambda row, col: load(row, col).wait())
        add_listed(plan, 0, jnp.minimum(n, KEEP), wide, lambda k: got[k], acc)
        fetch_more("wait")
        add_listed(plan, jnp.minimum(n, KEEP), n, wide, lambda k: got[k], acc)
        touched(lambda row, col: store(row, col).start())
        touched(lambda row, col: store(row, col).wait())


def late(side, plan, wide, kept_b, total, sides):
    edge = kept_b.shape[1]
    tile = plan.shape[1] - 1
    return pl.pallas_call(
        late_kernel,
        out_shape=jax.ShapeDtypeStruct(total.shape, total.dtype),
        in_specs=[SMEM] * 2 + [ANY] * 7,
        out_specs=ANY,
        input_output_aliases={4: 0},
        scratch_shapes=[
            pltpu.VMEM(total.shape, jnp.float32),
            pltpu.VMEM(wide.shape, wide.dtype),
            pltpu.VMEM((tile - FIRST, edge, edge), jnp.float32),
            pltpu.SMEM((RB * CB,), jnp.int32),
            pltpu.SemaphoreType.DMA((5,)),
        ],
        compiler_params=pltpu.CompilerParams(vmem_limit_bytes=GRANT),
        cost_estimate=cost(6 * tile * edge**3, 2 * total.size),
    )(side, plan, wide, kept_b, total, *sides)


def per_device(a_blocks, a_coords, b_blocks, b_coords):
    rows, cols = lax.axis_size("row"), lax.axis_size("col")
    per_col = rows // cols
    my_row, my_col = lax.axis_index("row"), lax.axis_index("col")
    a, a_pos, b, b_pos = a_blocks[0, 0], a_coords[0, 0], b_blocks[0, 0], b_coords[0, 0]
    count = a.shape[0] // per_col
    edge, tile = a.shape[1], b.shape[0]

    def send(x, pairs):
        flat = [(r * cols + c, s * cols + d) for (r, c), (s, d) in pairs]
        return lax.ppermute(x, ("row", "col"), flat)

    def ring(x):
        return lax.ppermute(x, "row", [((r + 1) % rows, r) for r in range(rows)])

    def owner(row, step):
        return (row + step) % rows // per_col

    everywhere = [(r, c) for r in range(rows) for c in range(cols)]
    swap = [((r, c), (r, c ^ 1)) for r, c in everywhere]

    note = jnp.pad(b_pos.astype(jnp.float32), ((0, NOTE - 2), (0, edge - tile)))
    first_b = jnp.concatenate([b[:FIRST].reshape(FIRST * edge, edge), note])
    first_b, a_pos = lax.optimization_barrier((first_b, a_pos))
    first_b = ring(first_b)
    next_pos = first_b[FIRST * edge : FIRST * edge + 2, :tile].astype(jnp.int32)
    asked = 0
    for d in range(0, cols, 2):
        pairs = [((r, owner(r, 1)), ((r + 1) % rows, (owner(r, 1) + d) % cols)) for r in range(rows)]
        asked = asked + send(a_pos, pairs)
    packed = pack(a_pos, a, count)
    got = 0
    for d in range(2, cols, 2):
        pairs = sorted({((r, owner(r, s)), (r, (owner(r, s) + d) % cols)) for r in range(rows) for s in range(STEPS)})
        got = got + send(packed, pairs)
    owners = [owner(my_row, s) for s in range(STEPS)]
    own = functools.reduce(jnp.logical_or, [my_col == o for o in owners])

    asked = asked + send(asked, swap)
    half = (my_row % per_col).astype(jnp.int32)
    keep_b, more_b, rest_b = select(half[None], asked, b_pos, b, (KEEP, MORE, tile - FIRST - KEEP - MORE))
    kept_b = ring(keep_b)

    got, _ = lax.optimization_barrier((got, keep_b))
    mine = jnp.where(own, packed, got)
    other = send(mine, swap)

    def notes_of(x):
        return x.reshape(per_col, -1, edge)[:, count * edge : count * edge + 2, :count].astype(jnp.int32)

    use, pos = [], []
    mine_notes, other_notes = notes_of(mine), notes_of(other)
    for s in range(STEPS):
        h, near = (my_row + s) % per_col, my_col % 2 == owners[s] % 2
        use += [h, near]
        pos.append(lax.dynamic_index_in_dim(jnp.where(near, mine_notes, other_notes), h, keepdims=False))
    use += [my_row % 2, half]
    use = jnp.stack([u.astype(jnp.int32) for u in use])

    total, wide, plan, code = early(first_b, (next_pos, asked, use, *pos, b_pos), mine, other, b)

    sides, code = [], jnp.maximum(code[0], 0)
    for parity in range(2):
        pairs = [(((r + 1) % rows, c), (r, c)) for r in range(parity, rows, 2) for c in range(cols)]

        def none():
            return empty((more_b.shape, rest_b.shape))

        def small():
            return send(more_b, pairs), *empty((rest_b.shape,))

        def full():
            return send(more_b, pairs), send(rest_b, pairs)

        which = jnp.bitwise_and(lax.shift_right_logical(code, 2 * parity), 3)
        sides += lax.switch(which, [none, small, full])

    side = (my_row % 2).astype(jnp.int32)[None]
    return late(side, plan, wide, kept_b, total, sides)


def solution(mesh):
    return jax.shard_map(
        per_device,
        mesh=mesh,
        in_specs=(
            P("row", "col", None, None, None),
            P("row", "col", None, None),
            P("row", "col", None, None, None),
            P("row", "col", None, None),
        ),
        out_specs=P("row", "col"),
        check_vma=False,
    )
```

```python
import functools

import jax
import jax.numpy as jnp
from jax import lax
from jax.experimental import pallas as pl
from jax.experimental.pallas import tpu as pltpu
from jax.sharding import PartitionSpec as P

KB = 32
RB = 2
CB = 16
STEPS = 2
FIRST = 6
KEEP = 8
MORE = 4
GRANT = 56 << 20
NOTE = 8

VMEM = pl.BlockSpec(memory_space=pltpu.VMEM)
SMEM = pl.BlockSpec(memory_space=pltpu.SMEM)
ANY = pl.BlockSpec(memory_space=pl.ANY)


def cost(flops, size):
    return pl.CostEstimate(flops=flops, bytes_accessed=4 * size, transcendentals=0)


def pack_kernel(count, pieces, pos_ref, a_ref, out_ref, sem):
    stored, edge = a_ref.shape[0], a_ref.shape[1]
    span = count * edge + NOTE
    lane = lax.broadcasted_iota(jnp.int32, (NOTE, edge), 1)
    line = lax.broadcasted_iota(jnp.int32, (NOTE, edge), 0)
    notes = [jnp.zeros((NOTE, edge), jnp.int32) for _ in range(pieces)]
    places = [jnp.int32(0) for _ in range(pieces)]
    for m in range(stored):
        row, col = pos_ref[0, m], pos_ref[1, m]
        piece = col // KB
        at = places[-1]
        for h in range(pieces - 1):
            at = jnp.where(piece == h, places[h], at)
        start = pl.multiple_of(piece * span + at * edge, 8)
        pltpu.make_async_copy(a_ref.at[m], out_ref.at[pl.ds(start, edge)], sem).start()
        for h in range(pieces):
            mine = piece == h
            hit = mine & (lane == at)
            notes[h] = jnp.where(hit & (line == 0), row, notes[h])
            notes[h] = jnp.where(hit & (line == 1), col % KB, notes[h])
            places[h] = places[h] + mine.astype(jnp.int32)
    for h in range(pieces):
        out_ref[pl.ds(h * span + count * edge, NOTE), :] = notes[h].astype(jnp.float32)
    for m in range(stored):
        pltpu.make_async_copy(a_ref.at[m], out_ref.at[pl.ds(m * edge, edge)], sem).wait()


def pack(pos, blocks, count):
    stored, edge = blocks.shape[:2]
    pieces = stored // count
    return pl.pallas_call(
        functools.partial(pack_kernel, count, pieces),
        out_shape=jax.ShapeDtypeStruct((pieces * (count * edge + NOTE), edge), jnp.float32),
        in_specs=[SMEM, ANY],
        out_specs=VMEM,
        scratch_shapes=[pltpu.SemaphoreType.DMA],
        compiler_params=pltpu.CompilerParams(vmem_limit_bytes=8 << 20),
        cost_estimate=cost(0, 2 * blocks.size),
    )(pos, blocks)


def select_kernel(half_ref, a_pos_ref, b_pos_ref, b_ref, keep_ref, more_ref, rest_ref, got, lut, index, sems):
    for k in range(KB):
        lut[k] = 0
    for m in range(a_pos_ref.shape[1]):

        @pl.when(a_pos_ref[1, m] // KB == half_ref[0])
        def _():
            lut[a_pos_ref[1, m] % KB] = 1

    n = jnp.int32(0)
    for m in range(FIRST, b_ref.shape[0]):
        index[n] = m
        n = n + lut[b_pos_ref[0, m]]

    def fetch(k):
        return pltpu.make_async_copy(b_ref.at[index[k]], got.at[k], sems.at[0])

    pl.loop(0, n)(lambda k: fetch(k).start())
    pl.loop(0, n)(lambda k: fetch(k).wait())
    for act in ("start", "wait"):
        for out, start, on in (
            (keep_ref, 0, n > 0),
            (more_ref, KEEP, (n > KEEP) & (n <= KEEP + MORE)),
            (rest_ref, KEEP, n > KEEP + MORE),
        ):

            @pl.when(on)
            def _():
                getattr(pltpu.make_async_copy(got.at[pl.ds(start, out.shape[0])], out, sems.at[1]), act)()


def select(half, a_pos, b_pos, b):
    tile = b.shape[0]
    sizes = (KEEP, MORE, tile - FIRST - KEEP)
    return pl.pallas_call(
        select_kernel,
        out_shape=tuple(jax.ShapeDtypeStruct((n,) + b.shape[1:], b.dtype) for n in sizes),
        in_specs=[SMEM, SMEM, SMEM, ANY],
        out_specs=(ANY,) * len(sizes),
        scratch_shapes=[
            pltpu.VMEM((tile - FIRST,) + b.shape[1:], b.dtype),
            pltpu.SMEM((KB,), jnp.int32),
            pltpu.SMEM((tile + 1,), jnp.int32),
            pltpu.SemaphoreType.DMA((2,)),
        ],
        compiler_params=pltpu.CompilerParams(vmem_limit_bytes=GRANT),
        cost_estimate=cost(0, b.size),
    )(half, a_pos, b_pos, b)


def split(x):
    high = x.astype(jnp.bfloat16)
    return high, (x - high.astype(jnp.float32)).astype(jnp.bfloat16)


def product(a_wide, b):
    high, low = split(b)
    wide = jnp.concatenate(
        [jnp.concatenate([high, low], axis=1), jnp.concatenate([high, jnp.zeros_like(low)], axis=1)], axis=0
    )
    both = jnp.dot(a_wide, wide, preferred_element_type=jnp.float32)
    edge = b.shape[1]
    return both[:, :edge] + both[:, edge:]


def listed(lut, lists, a_pos_ref, b_pos_ref, first, stop):
    for k in range(KB):
        lut[k] = -1
    for m in range(a_pos_ref.shape[1]):
        lut[a_pos_ref[1, m]] = m
    n = jnp.int32(0)
    for m in range(first, stop):
        which = lut[b_pos_ref[0, m]]
        lists[0, n] = which
        lists[1, n] = a_pos_ref[0, jnp.maximum(which, 0)]
        lists[2, n] = b_pos_ref[1, m]
        lists[3, n] = m
        n = n + (which >= 0).astype(jnp.int32)
    return n


def add_listed(lists, low, high, a_wide, b_block, out_ref, after=None):
    edge = a_wide.shape[1]

    def one(n):
        return product(a_wide[lists[0, n]], b_block(n))

    def put(n, part):
        row = pl.multiple_of(lists[1, n] * edge, edge)
        col = pl.multiple_of(lists[2, n] * edge, edge)
        out_ref[pl.ds(row, edge), pl.ds(col, edge)] += part
        if after is not None:
            after(n)

    pairs = jnp.maximum(high - low, 0) // 2

    @pl.loop(0, pairs)
    def _(t):
        n = low + 2 * t
        parts = one(n), one(n + 1)
        put(n, parts[0])
        put(n + 1, parts[1])

    @pl.when(low + 2 * pairs < high)
    def _():
        put(high - 1, one(high - 1))


def widen(a_wide, x):
    count, edge = a_wide.shape[:2]
    for m in range(count):
        high, low = split(x[pl.ds(m * edge, edge), :])
        a_wide[m, :, :edge] = high
        a_wide[m, :, edge:] = low


def spot(ref, edge, row, col):
    rows = pl.ds(pl.multiple_of(row * edge, edge), edge)
    return ref.at[rows, pl.ds(pl.multiple_of(col * edge, edge), edge)]


def level(n):
    return (n > KEEP).astype(jnp.int32) + (n > KEEP + MORE).astype(jnp.int32)


def early_kernel(*refs):
    (first_ref, next_pos_ref, asked_ref, use_ref, pos0_ref, pos1_ref, b_pos_ref), refs = refs[:7], refs[7:]
    mine_ref, other_ref, b_ref, out_ref, wide_out, plan, code_ref, *refs = refs
    acc, nought, x0, x1, b_v, first_v, wide0, wide1, lut, lists, firsts, seen, sems = refs
    sem, wide_copy = sems.at[0], pltpu.make_async_copy(wide1, wide_out, sems.at[1])
    count, edge = wide0.shape[:2]
    tile = b_pos_ref.shape[1]
    span = count * edge + NOTE

    def load(s, src, x):
        start = pl.multiple_of(use_ref[2 * s] * span, 8)
        return pltpu.make_async_copy(src.at[pl.ds(start, count * edge)], x, sems.at[2 + s])

    for s, x in enumerate((x0, x1)):
        for src, on in ((mine_ref, 1), (other_ref, 0)):

            @pl.when(use_ref[2 * s + 1] == on)
            def _():
                load(s, src, x).start()

    def block(k):
        return pltpu.make_async_copy(b_ref.at[lists[3, k]], b_v.at[k], sems.at[4])

    def early_block(k):
        start = pl.multiple_of(firsts[3, k] * edge, edge)
        return pltpu.make_async_copy(first_ref.at[pl.ds(start, edge)], first_v.at[k], sems.at[5])

    n = listed(lut, lists, pos0_ref, b_pos_ref, 0, tile)
    pl.loop(0, n)(lambda k: block(k).start())
    n1 = listed(lut, firsts, pos1_ref, next_pos_ref, 0, FIRST)
    pl.loop(0, n1)(lambda k: early_block(k).start())
    for k in range(RB * CB):
        seen[k] = 0
    nought[...] = jnp.zeros_like(nought)

    def touch(list_ref):
        def act(k):
            row, col = list_ref[1, k], list_ref[2, k]
            seen[row * CB + col] = 1
            spot(acc, edge, row, col)[...] = nought[...]

        return act

    pl.loop(0, n)(touch(lists))
    pl.loop(0, n1)(touch(firsts))
    for row in range(RB):
        for col in range(CB):

            @pl.when(seen[row * CB + col] == 0)
            def _():
                pltpu.make_async_copy(nought, spot(out_ref, edge, row, col), sem).start()

    load(1, mine_ref, x1).wait()
    widen(wide1, x1)
    wide_copy.start()
    load(0, mine_ref, x0).wait()
    widen(wide0, x0)
    pl.loop(0, n)(lambda k: block(k).wait())
    add_listed(lists, 0, n, wide0, lambda k: b_v[k], acc)
    pl.loop(0, n1)(lambda k: early_block(k).wait())
    add_listed(firsts, 0, n1, wide1, lambda k: first_v[k], acc)
    for row in range(RB):
        for col in range(CB):

            @pl.when(seen[row * CB + col] == 1)
            def _():
                pltpu.make_async_copy(spot(acc, edge, row, col), spot(out_ref, edge, row, col), sem).start()

    gets = listed(lut, plan, pos1_ref, next_pos_ref, FIRST, tile)
    plan[0, tile] = gets
    for k in range(KB):
        lut[k] = 0
    for m in range(asked_ref.shape[1]):

        @pl.when(asked_ref[1, m] // KB == use_ref[2 * STEPS + 1])
        def _():
            lut[asked_ref[1, m] % KB] = 1

    gives = jnp.int32(0)
    for m in range(FIRST, tile):
        gives = gives + lut[b_pos_ref[0, m]]
    even = use_ref[2 * STEPS] == 0
    code_ref[0] = level(jnp.where(even, gets, gives)) + 4 * level(jnp.where(even, gives, gets))
    pltpu.make_async_copy(acc, out_ref, sem).wait()
    wide_copy.wait()


def early(first_b, coords, mine, other, b):
    tile, edge = b.shape[:2]
    count = coords[3].shape[1]
    wide = (count, edge, 2 * edge)
    total = (RB * edge, CB * edge)
    return pl.pallas_call(
        early_kernel,
        out_shape=(
            jax.ShapeDtypeStruct(total, jnp.float32),
            jax.ShapeDtypeStruct(wide, jnp.bfloat16),
            jax.ShapeDtypeStruct((4, tile + 1), jnp.int32),
            jax.ShapeDtypeStruct((1,), jnp.int32),
        ),
        in_specs=[ANY] + [SMEM] * len(coords) + [ANY] * 3,
        out_specs=(ANY, ANY, SMEM, SMEM),
        scratch_shapes=[
            pltpu.VMEM(total, jnp.float32),
            pltpu.VMEM((edge, edge), jnp.float32),
            pltpu.VMEM((count * edge, edge), jnp.float32),
            pltpu.VMEM((count * edge, edge), jnp.float32),
            pltpu.VMEM(b.shape, jnp.float32),
            pltpu.VMEM((FIRST, edge, edge), jnp.float32),
            pltpu.VMEM(wide, jnp.bfloat16),
            pltpu.VMEM(wide, jnp.bfloat16),
            pltpu.SMEM((KB,), jnp.int32),
            pltpu.SMEM((4, tile + 1), jnp.int32),
            pltpu.SMEM((4, tile + 1), jnp.int32),
            pltpu.SMEM((RB * CB,), jnp.int32),
            pltpu.SemaphoreType.DMA((6,)),
        ],
        compiler_params=pltpu.CompilerParams(vmem_limit_bytes=GRANT),
        cost_estimate=cost(6 * b.size * edge, 2 * b.size),
    )(first_b, *coords, mine, other, b)


def empty(shapes):
    return pl.pallas_call(
        lambda *refs: None,
        out_shape=tuple(jax.ShapeDtypeStruct(x, jnp.float32) for x in shapes),
        out_specs=(ANY,) * len(shapes),
    )()


def late_kernel(side_ref, plan, wide_ref, kept_ref, total_ref, *refs):
    sides, (out_ref, acc, wide, got, seen, sems) = refs[:4], refs[4:]
    edge = wide.shape[1]
    tile = plan.shape[1] - 1
    n = plan[0, tile]

    def load(row, col):
        return pltpu.make_async_copy(spot(out_ref, edge, row, col), spot(acc, edge, row, col), sems.at[2])

    def store(row, col):
        return pltpu.make_async_copy(spot(acc, edge, row, col), spot(out_ref, edge, row, col), sems.at[3])

    def touched(act):
        for row in range(RB):
            for col in range(CB):

                @pl.when(seen[row * CB + col] > 0)
                def _():
                    act(row, col)

    @pl.when(n > 0)
    def _():
        def fetch(act):
            getattr(pltpu.make_async_copy(wide_ref, wide, sems.at[4]), act)()
            getattr(pltpu.make_async_copy(kept_ref, got.at[pl.ds(0, KEEP)], sems.at[0]), act)()

        def fetch_more(act):
            for side in range(2):
                more, rest = sides[2 * side : 2 * side + 2]
                for src, on in ((more, (n > KEEP) & (n <= KEEP + MORE)), (rest, n > KEEP + MORE)):

                    @pl.when((side_ref[0] == side) & on)
                    def _():
                        getattr(pltpu.make_async_copy(src, got.at[pl.ds(KEEP, src.shape[0])], sems.at[1]), act)()

        fetch("start")
        for k in range(RB * CB):
            seen[k] = 0

        @pl.loop(0, n)
        def _(k):
            row, col = plan[1, k], plan[2, k]

            @pl.when(seen[row * CB + col] == 0)
            def _():
                load(row, col).start()

            seen[row * CB + col] = k + 1

        fetch_more("start")
        fetch("wait")
        touched(lambda row, col: load(row, col).wait())

        def after(k):
            row, col = plan[1, k], plan[2, k]

            @pl.when(seen[row * CB + col] == k + 1)
            def _():
                store(row, col).start()

        add_listed(plan, 0, jnp.minimum(n, KEEP), wide, lambda k: got[k], acc, after)
        fetch_more("wait")
        add_listed(plan, jnp.minimum(n, KEEP), n, wide, lambda k: got[k], acc, after)
        touched(lambda row, col: store(row, col).wait())


def late(side, plan, wide, kept_b, total, sides):
    edge = kept_b.shape[1]
    tile = plan.shape[1] - 1
    return pl.pallas_call(
        late_kernel,
        out_shape=jax.ShapeDtypeStruct(total.shape, total.dtype),
        in_specs=[SMEM] * 2 + [ANY] * 7,
        out_specs=ANY,
        input_output_aliases={4: 0},
        scratch_shapes=[
            pltpu.VMEM(total.shape, jnp.float32),
            pltpu.VMEM(wide.shape, wide.dtype),
            pltpu.VMEM((tile - FIRST, edge, edge), jnp.float32),
            pltpu.SMEM((RB * CB,), jnp.int32),
            pltpu.SemaphoreType.DMA((5,)),
        ],
        compiler_params=pltpu.CompilerParams(vmem_limit_bytes=GRANT),
        cost_estimate=cost(6 * tile * edge**3, 2 * total.size),
    )(side, plan, wide, kept_b, total, *sides)


def per_device(a_blocks, a_coords, b_blocks, b_coords):
    rows, cols = lax.axis_size("row"), lax.axis_size("col")
    per_col = rows // cols
    my_row, my_col = lax.axis_index("row"), lax.axis_index("col")
    a, a_pos, b, b_pos = a_blocks[0, 0], a_coords[0, 0], b_blocks[0, 0], b_coords[0, 0]
    count = a.shape[0] // per_col
    edge, tile = a.shape[1], b.shape[0]

    def send(x, pairs):
        flat = [(r * cols + c, s * cols + d) for (r, c), (s, d) in pairs]
        return lax.ppermute(x, ("row", "col"), flat)

    def ring(x):
        return lax.ppermute(x, "row", [((r + 1) % rows, r) for r in range(rows)])

    def owner(row, step):
        return (row + step) % rows // per_col

    everywhere = [(r, c) for r in range(rows) for c in range(cols)]
    swap = [((r, c), (r, c ^ 1)) for r, c in everywhere]

    note = jnp.pad(b_pos.astype(jnp.float32), ((0, NOTE - 2), (0, edge - tile)))
    first_b = jnp.concatenate([b[:FIRST].reshape(FIRST * edge, edge), note])
    first_b, a_pos = lax.optimization_barrier((first_b, a_pos))
    first_b = ring(first_b)
    next_pos = first_b[FIRST * edge : FIRST * edge + 2, :tile].astype(jnp.int32)
    asked = 0
    for d in range(0, cols, 2):
        pairs = [((r, owner(r, 1)), ((r + 1) % rows, (owner(r, 1) + d) % cols)) for r in range(rows)]
        asked = asked + send(a_pos, pairs)
    packed = pack(a_pos, a, count)
    got = 0
    for d in range(2, cols, 2):
        pairs = sorted({((r, owner(r, s)), (r, (owner(r, s) + d) % cols)) for r in range(rows) for s in range(STEPS)})
        got = got + send(packed, pairs)
    owners = [owner(my_row, s) for s in range(STEPS)]
    own = functools.reduce(jnp.logical_or, [my_col == o for o in owners])

    asked = asked + send(asked, swap)
    half = (my_row % per_col).astype(jnp.int32)
    keep_b, more_b, rest_b = select(half[None], asked, b_pos, b)
    kept_b = ring(keep_b)

    got, _ = lax.optimization_barrier((got, keep_b))
    mine = jnp.where(own, packed, got)
    other = send(mine, swap)

    def notes_of(x):
        return x.reshape(per_col, -1, edge)[:, count * edge : count * edge + 2, :count].astype(jnp.int32)

    use, pos = [], []
    mine_notes, other_notes = notes_of(mine), notes_of(other)
    for s in range(STEPS):
        h, near = (my_row + s) % per_col, my_col % 2 == owners[s] % 2
        use += [h, near]
        pos.append(lax.dynamic_index_in_dim(jnp.where(near, mine_notes, other_notes), h, keepdims=False))
    use += [my_row % 2, half]
    use = jnp.stack([u.astype(jnp.int32) for u in use])

    total, wide, plan, code = early(first_b, (next_pos, asked, use, *pos, b_pos), mine, other, b)

    sides, code = [], jnp.maximum(code[0], 0)
    for parity in range(2):
        pairs = [(((r + 1) % rows, c), (r, c)) for r in range(parity, rows, 2) for c in range(cols)]

        def none():
            return empty((more_b.shape, rest_b.shape))

        def small():
            return send(more_b, pairs), *empty((rest_b.shape,))

        def full():
            return *empty((more_b.shape,)), send(rest_b, pairs)

        which = jnp.bitwise_and(lax.shift_right_logical(code, 2 * parity), 3)
        sides += lax.switch(which, [none, small, full])

    side = (my_row % 2).astype(jnp.int32)[None]
    return late(side, plan, wide, kept_b, total, sides)


def solution(mesh):
    return jax.shard_map(
        per_device,
        mesh=mesh,
        in_specs=(
            P("row", "col", None, None, None),
            P("row", "col", None, None),
            P("row", "col", None, None, None),
            P("row", "col", None, None),
        ),
        out_specs=P("row", "col"),
        check_vma=False,
    )
```

```python
import functools

import jax
import jax.numpy as jnp
from jax import lax
from jax.experimental import pallas as pl
from jax.experimental.pallas import tpu as pltpu
from jax.sharding import PartitionSpec as P

KB = 32
RB = 2
CB = 16
STEPS = 2
FIRST = 6
KEEP = 8
MORE = 4
GRANT = 56 << 20
NOTE = 8

VMEM = pl.BlockSpec(memory_space=pltpu.VMEM)
SMEM = pl.BlockSpec(memory_space=pltpu.SMEM)
ANY = pl.BlockSpec(memory_space=pl.ANY)


def cost(flops, size):
    return pl.CostEstimate(flops=flops, bytes_accessed=4 * size, transcendentals=0)


def pack_kernel(count, pieces, pos_ref, a_ref, out_ref, sem):
    stored, edge = a_ref.shape[0], a_ref.shape[1]
    span = count * edge + NOTE
    lane = lax.broadcasted_iota(jnp.int32, (NOTE, edge), 1)
    line = lax.broadcasted_iota(jnp.int32, (NOTE, edge), 0)
    notes = [jnp.zeros((NOTE, edge), jnp.int32) for _ in range(pieces)]
    places = [jnp.int32(0) for _ in range(pieces)]
    for m in range(stored):
        row, col = pos_ref[0, m], pos_ref[1, m]
        piece = col // KB
        at = places[-1]
        for h in range(pieces - 1):
            at = jnp.where(piece == h, places[h], at)
        start = pl.multiple_of(piece * span + at * edge, 8)
        pltpu.make_async_copy(a_ref.at[m], out_ref.at[pl.ds(start, edge)], sem).start()
        for h in range(pieces):
            mine = piece == h
            hit = mine & (lane == at)
            notes[h] = jnp.where(hit & (line == 0), row, notes[h])
            notes[h] = jnp.where(hit & (line == 1), col % KB, notes[h])
            places[h] = places[h] + mine.astype(jnp.int32)
    for h in range(pieces):
        out_ref[pl.ds(h * span + count * edge, NOTE), :] = notes[h].astype(jnp.float32)
    for m in range(stored):
        pltpu.make_async_copy(a_ref.at[m], out_ref.at[pl.ds(m * edge, edge)], sem).wait()


def pack(pos, blocks, count):
    stored, edge = blocks.shape[:2]
    pieces = stored // count
    return pl.pallas_call(
        functools.partial(pack_kernel, count, pieces),
        out_shape=jax.ShapeDtypeStruct((pieces * (count * edge + NOTE), edge), jnp.float32),
        in_specs=[SMEM, ANY],
        out_specs=VMEM,
        scratch_shapes=[pltpu.SemaphoreType.DMA],
        compiler_params=pltpu.CompilerParams(vmem_limit_bytes=8 << 20),
        cost_estimate=cost(0, 2 * blocks.size),
    )(pos, blocks)


def select_kernel(half_ref, here_ref, there_ref, b_pos_ref, b_ref, keep_ref, more_ref, rest_ref, got, lut, index, sems):
    for k in range(KB):
        lut[k] = 0
    for m in range(here_ref.shape[1]):
        column = here_ref[1, m] + there_ref[1, m]

        @pl.when(column // KB == half_ref[0])
        def _():
            lut[column % KB] = 1

    n = jnp.int32(0)
    for m in range(FIRST, b_ref.shape[0]):
        index[n] = m
        n = n + lut[b_pos_ref[0, m]]

    def fetch(k):
        return pltpu.make_async_copy(b_ref.at[index[k]], got.at[k], sems.at[0])

    pl.loop(0, n)(lambda k: fetch(k).start())
    pl.loop(0, n)(lambda k: fetch(k).wait())
    for act in ("start", "wait"):
        for out, start, on in (
            (keep_ref, 0, n > 0),
            (more_ref, KEEP, (n > KEEP) & (n <= KEEP + MORE)),
            (rest_ref, KEEP, n > KEEP + MORE),
        ):

            @pl.when(on)
            def _():
                getattr(pltpu.make_async_copy(got.at[pl.ds(start, out.shape[0])], out, sems.at[1]), act)()


def select(half, asked, b_pos, b):
    tile = b.shape[0]
    sizes = (KEEP, MORE, tile - FIRST - KEEP)
    return pl.pallas_call(
        select_kernel,
        out_shape=tuple(jax.ShapeDtypeStruct((n,) + b.shape[1:], b.dtype) for n in sizes),
        in_specs=[SMEM] * 4 + [ANY],
        out_specs=(ANY,) * len(sizes),
        scratch_shapes=[
            pltpu.VMEM((tile - FIRST,) + b.shape[1:], b.dtype),
            pltpu.SMEM((KB,), jnp.int32),
            pltpu.SMEM((tile + 1,), jnp.int32),
            pltpu.SemaphoreType.DMA((2,)),
        ],
        compiler_params=pltpu.CompilerParams(vmem_limit_bytes=GRANT),
        cost_estimate=cost(0, b.size),
    )(half, *asked, b_pos, b)


def split(x):
    high = x.astype(jnp.bfloat16)
    return high, (x - high.astype(jnp.float32)).astype(jnp.bfloat16)


def product(a_wide, b):
    high, low = split(b)
    wide = jnp.concatenate(
        [jnp.concatenate([high, low], axis=1), jnp.concatenate([high, jnp.zeros_like(low)], axis=1)], axis=0
    )
    both = jnp.dot(a_wide, wide, preferred_element_type=jnp.float32)
    edge = b.shape[1]
    return both[:, :edge] + both[:, edge:]


def listed(lut, lists, a_pos_ref, b_pos_ref, first, stop):
    for k in range(KB):
        lut[k] = -1
    for m in range(a_pos_ref.shape[1]):
        lut[a_pos_ref[1, m]] = m
    n = jnp.int32(0)
    for m in range(first, stop):
        which = lut[b_pos_ref[0, m]]
        lists[0, n] = which
        lists[1, n] = a_pos_ref[0, jnp.maximum(which, 0)]
        lists[2, n] = b_pos_ref[1, m]
        lists[3, n] = m
        n = n + (which >= 0).astype(jnp.int32)
    return n


def add_listed(lists, low, high, a_wide, b_block, out_ref, after=None):
    edge = a_wide.shape[1]

    def one(n):
        return product(a_wide[lists[0, n]], b_block(n))

    def put(n, part):
        row = pl.multiple_of(lists[1, n] * edge, edge)
        col = pl.multiple_of(lists[2, n] * edge, edge)
        out_ref[pl.ds(row, edge), pl.ds(col, edge)] += part
        if after is not None:
            after(n)

    pairs = jnp.maximum(high - low, 0) // 2

    @pl.loop(0, pairs)
    def _(t):
        n = low + 2 * t
        parts = one(n), one(n + 1)
        put(n, parts[0])
        put(n + 1, parts[1])

    @pl.when(low + 2 * pairs < high)
    def _():
        put(high - 1, one(high - 1))


def widen(a_wide, x):
    count, edge = a_wide.shape[:2]
    for m in range(count):
        high, low = split(x[pl.ds(m * edge, edge), :])
        a_wide[m, :, :edge] = high
        a_wide[m, :, edge:] = low


def spot(ref, edge, row, col):
    rows = pl.ds(pl.multiple_of(row * edge, edge), edge)
    return ref.at[rows, pl.ds(pl.multiple_of(col * edge, edge), edge)]


def level(n):
    return (n > KEEP).astype(jnp.int32) + (n > KEEP + MORE).astype(jnp.int32)


def early_kernel(rows, cols, *refs):
    (first_ref, next_pos_ref, here_ref, there_ref, pos0_ref, pos1_ref, b_pos_ref), refs = refs[:7], refs[7:]
    my_row, my_col = lax.axis_index("row"), lax.axis_index("col")
    tiles = [lax.rem(my_row + s, rows) for s in range(STEPS)]
    halves = [lax.rem(tile, rows // cols) for tile in tiles]
    near = [lax.rem(my_col, 2) == lax.rem(tile // (rows // cols), 2) for tile in tiles]
    mine_ref, other_ref, b_ref, out_ref, wide_out, plan, code_ref, *refs = refs
    acc, nought, x0, x1, b_v, first_v, wide0, wide1, lut, lists, firsts, seen, sems = refs
    sem, wide_copy = sems.at[0], pltpu.make_async_copy(wide1, wide_out, sems.at[1])
    count, edge = wide0.shape[:2]
    tile = b_pos_ref.shape[1]
    span = count * edge + NOTE

    def load(s, src, x):
        start = pl.multiple_of(halves[s] * span, 8)
        return pltpu.make_async_copy(src.at[pl.ds(start, count * edge)], x, sems.at[2 + s])

    for s, x in enumerate((x0, x1)):
        for src, on in ((mine_ref, near[s]), (other_ref, jnp.logical_not(near[s]))):

            @pl.when(on)
            def _():
                load(s, src, x).start()

    def block(k):
        return pltpu.make_async_copy(b_ref.at[lists[3, k]], b_v.at[k], sems.at[4])

    def early_block(k):
        start = pl.multiple_of(firsts[3, k] * edge, edge)
        return pltpu.make_async_copy(first_ref.at[pl.ds(start, edge)], first_v.at[k], sems.at[5])

    n = listed(lut, lists, pos0_ref, b_pos_ref, 0, tile)
    pl.loop(0, n)(lambda k: block(k).start())
    n1 = listed(lut, firsts, pos1_ref, next_pos_ref, 0, FIRST)
    pl.loop(0, n1)(lambda k: early_block(k).start())
    for k in range(RB * CB):
        seen[k] = 0
    nought[...] = jnp.zeros_like(nought)

    def touch(list_ref):
        def act(k):
            row, col = list_ref[1, k], list_ref[2, k]
            seen[row * CB + col] = 1
            spot(acc, edge, row, col)[...] = nought[...]

        return act

    pl.loop(0, n)(touch(lists))
    pl.loop(0, n1)(touch(firsts))
    for row in range(RB):
        for col in range(CB):

            @pl.when(seen[row * CB + col] == 0)
            def _():
                pltpu.make_async_copy(nought, spot(out_ref, edge, row, col), sem).start()

    load(1, mine_ref, x1).wait()
    widen(wide1, x1)
    wide_copy.start()
    load(0, mine_ref, x0).wait()
    widen(wide0, x0)
    pl.loop(0, n)(lambda k: block(k).wait())
    add_listed(lists, 0, n, wide0, lambda k: b_v[k], acc)
    pl.loop(0, n1)(lambda k: early_block(k).wait())
    add_listed(firsts, 0, n1, wide1, lambda k: first_v[k], acc)
    for row in range(RB):
        for col in range(CB):

            @pl.when(seen[row * CB + col] == 1)
            def _():
                pltpu.make_async_copy(spot(acc, edge, row, col), spot(out_ref, edge, row, col), sem).start()

    gets = listed(lut, plan, pos1_ref, next_pos_ref, FIRST, tile)
    plan[0, tile] = gets
    for k in range(KB):
        lut[k] = 0
    for m in range(here_ref.shape[1]):
        column = here_ref[1, m] + there_ref[1, m]

        @pl.when(column // KB == halves[0])
        def _():
            lut[column % KB] = 1

    gives = jnp.int32(0)
    for m in range(FIRST, tile):
        gives = gives + lut[b_pos_ref[0, m]]
    even = lax.rem(my_row, 2) == 0
    code_ref[0] = level(jnp.where(even, gets, gives)) + 4 * level(jnp.where(even, gives, gets))
    pltpu.make_async_copy(acc, out_ref, sem).wait()
    wide_copy.wait()


def early(rows, cols, first_b, coords, mine, other, b):
    tile, edge = b.shape[:2]
    count = coords[3].shape[1]
    wide = (count, edge, 2 * edge)
    total = (RB * edge, CB * edge)
    return pl.pallas_call(
        functools.partial(early_kernel, rows, cols),
        out_shape=(
            jax.ShapeDtypeStruct(total, jnp.float32),
            jax.ShapeDtypeStruct(wide, jnp.bfloat16),
            jax.ShapeDtypeStruct((4, tile + 1), jnp.int32),
            jax.ShapeDtypeStruct((1,), jnp.int32),
        ),
        in_specs=[ANY] + [SMEM] * len(coords) + [ANY] * 3,
        out_specs=(ANY, ANY, SMEM, SMEM),
        scratch_shapes=[
            pltpu.VMEM(total, jnp.float32),
            pltpu.VMEM((edge, edge), jnp.float32),
            pltpu.VMEM((count * edge, edge), jnp.float32),
            pltpu.VMEM((count * edge, edge), jnp.float32),
            pltpu.VMEM(b.shape, jnp.float32),
            pltpu.VMEM((FIRST, edge, edge), jnp.float32),
            pltpu.VMEM(wide, jnp.bfloat16),
            pltpu.VMEM(wide, jnp.bfloat16),
            pltpu.SMEM((KB,), jnp.int32),
            pltpu.SMEM((4, tile + 1), jnp.int32),
            pltpu.SMEM((4, tile + 1), jnp.int32),
            pltpu.SMEM((RB * CB,), jnp.int32),
            pltpu.SemaphoreType.DMA((6,)),
        ],
        compiler_params=pltpu.CompilerParams(vmem_limit_bytes=GRANT),
        cost_estimate=cost(6 * b.size * edge, 2 * b.size),
    )(first_b, *coords, mine, other, b)


def empty(shapes):
    return pl.pallas_call(
        lambda *refs: None,
        out_shape=tuple(jax.ShapeDtypeStruct(x, jnp.float32) for x in shapes),
        out_specs=(ANY,) * len(shapes),
    )()


def late_kernel(side_ref, plan, wide_ref, kept_ref, total_ref, *refs):
    sides, (out_ref, acc, wide, got, seen, sems) = refs[:4], refs[4:]
    edge = wide.shape[1]
    tile = plan.shape[1] - 1
    n = plan[0, tile]

    def load(row, col):
        return pltpu.make_async_copy(spot(out_ref, edge, row, col), spot(acc, edge, row, col), sems.at[2])

    def store(row, col):
        return pltpu.make_async_copy(spot(acc, edge, row, col), spot(out_ref, edge, row, col), sems.at[3])

    def touched(act):
        for row in range(RB):
            for col in range(CB):

                @pl.when(seen[row * CB + col] > 0)
                def _():
                    act(row, col)

    @pl.when(n > 0)
    def _():
        def fetch(act):
            getattr(pltpu.make_async_copy(wide_ref, wide, sems.at[4]), act)()
            getattr(pltpu.make_async_copy(kept_ref, got.at[pl.ds(0, KEEP)], sems.at[0]), act)()

        def fetch_more(act):
            for side in range(2):
                more, rest = sides[2 * side : 2 * side + 2]
                for src, on in ((more, (n > KEEP) & (n <= KEEP + MORE)), (rest, n > KEEP + MORE)):

                    @pl.when((side_ref[0] == side) & on)
                    def _():
                        getattr(pltpu.make_async_copy(src, got.at[pl.ds(KEEP, src.shape[0])], sems.at[1]), act)()

        fetch("start")
        for k in range(RB * CB):
            seen[k] = 0

        @pl.loop(0, n)
        def _(k):
            row, col = plan[1, k], plan[2, k]

            @pl.when(seen[row * CB + col] == 0)
            def _():
                load(row, col).start()

            seen[row * CB + col] = k + 1

        fetch_more("start")
        fetch("wait")
        touched(lambda row, col: load(row, col).wait())

        def after(k):
            row, col = plan[1, k], plan[2, k]

            @pl.when(seen[row * CB + col] == k + 1)
            def _():
                store(row, col).start()

        add_listed(plan, 0, jnp.minimum(n, KEEP), wide, lambda k: got[k], acc, after)
        fetch_more("wait")
        add_listed(plan, jnp.minimum(n, KEEP), n, wide, lambda k: got[k], acc, after)
        touched(lambda row, col: store(row, col).wait())


def late(side, plan, wide, kept_b, total, sides):
    edge = kept_b.shape[1]
    tile = plan.shape[1] - 1
    return pl.pallas_call(
        late_kernel,
        out_shape=jax.ShapeDtypeStruct(total.shape, total.dtype),
        in_specs=[SMEM] * 2 + [ANY] * 7,
        out_specs=ANY,
        input_output_aliases={4: 0},
        scratch_shapes=[
            pltpu.VMEM(total.shape, jnp.float32),
            pltpu.VMEM(wide.shape, wide.dtype),
            pltpu.VMEM((tile - FIRST, edge, edge), jnp.float32),
            pltpu.SMEM((RB * CB,), jnp.int32),
            pltpu.SemaphoreType.DMA((5,)),
        ],
        compiler_params=pltpu.CompilerParams(vmem_limit_bytes=12 << 20),
        cost_estimate=cost(6 * tile * edge**3, 2 * total.size),
    )(side, plan, wide, kept_b, total, *sides)


def per_device(a_blocks, a_coords, b_blocks, b_coords):
    rows, cols = lax.axis_size("row"), lax.axis_size("col")
    per_col = rows // cols
    my_row, my_col = lax.axis_index("row"), lax.axis_index("col")
    a, a_pos, b, b_pos = a_blocks[0, 0], a_coords[0, 0], b_blocks[0, 0], b_coords[0, 0]
    count = a.shape[0] // per_col
    edge, tile = a.shape[1], b.shape[0]

    def send(x, pairs):
        flat = [(r * cols + c, s * cols + d) for (r, c), (s, d) in pairs]
        return lax.ppermute(x, ("row", "col"), flat)

    def ring(x):
        return lax.ppermute(x, "row", [((r + 1) % rows, r) for r in range(rows)])

    def owner(row, step):
        return (row + step) % rows // per_col

    everywhere = [(r, c) for r in range(rows) for c in range(cols)]
    swap = [((r, c), (r, c ^ 1)) for r, c in everywhere]

    note = jnp.pad(b_pos.astype(jnp.float32), ((0, NOTE - 2), (0, edge - tile)))
    first_b = jnp.concatenate([b[:FIRST].reshape(FIRST * edge, edge), note])
    first_b, a_pos = lax.optimization_barrier((first_b, a_pos))
    first_b = ring(first_b)
    next_pos = first_b[FIRST * edge : FIRST * edge + 2, :tile].astype(jnp.int32)
    asked = 0
    for d in range(0, cols, 2):
        pairs = [((r, owner(r, 1)), ((r + 1) % rows, (owner(r, 1) + d) % cols)) for r in range(rows)]
        asked = asked + send(a_pos, pairs)
    packed = pack(a_pos, a, count)
    got = 0
    for d in range(2, cols, 2):
        pairs = sorted({((r, owner(r, s)), (r, (owner(r, s) + d) % cols)) for r in range(rows) for s in range(STEPS)})
        got = got + send(packed, pairs)
    owners = [owner(my_row, s) for s in range(STEPS)]
    own = functools.reduce(jnp.logical_or, [my_col == o for o in owners])

    asked = asked, send(asked, swap)
    half = (my_row % per_col).astype(jnp.int32)
    keep_b, more_b, rest_b = select(half[None], asked, b_pos, b)
    kept_b = ring(keep_b)

    got, _ = lax.optimization_barrier((got, keep_b))
    mine = jnp.where(own, packed, got)
    other = send(mine, swap)

    def notes_of(x):
        return x.reshape(per_col, -1, edge)[:, count * edge : count * edge + 2, :count].astype(jnp.int32)

    pos = []
    mine_notes, other_notes = notes_of(mine), notes_of(other)
    for s in range(STEPS):
        h, near = (my_row + s) % per_col, my_col % 2 == owners[s] % 2
        pos.append(lax.dynamic_index_in_dim(jnp.where(near, mine_notes, other_notes), h, keepdims=False))

    total, wide, plan, code = early(rows, cols, first_b, (next_pos, *asked, *pos, b_pos), mine, other, b)

    sides, code = [], jnp.maximum(code[0], 0)
    for parity in range(2):
        pairs = [(((r + 1) % rows, c), (r, c)) for r in range(parity, rows, 2) for c in range(cols)]

        def none():
            return empty((more_b.shape, rest_b.shape))

        def small():
            return send(more_b, pairs), *empty((rest_b.shape,))

        def full():
            return *empty((more_b.shape,)), send(rest_b, pairs)

        which = jnp.bitwise_and(lax.shift_right_logical(code, 2 * parity), 3)
        sides += lax.switch(which, [none, small, full])

    side = (my_row % 2).astype(jnp.int32)[None]
    return late(side, plan, wide, kept_b, total, sides)


def solution(mesh):
    return jax.shard_map(
        per_device,
        mesh=mesh,
        in_specs=(
            P("row", "col", None, None, None),
            P("row", "col", None, None),
            P("row", "col", None, None, None),
            P("row", "col", None, None),
        ),
        out_specs=P("row", "col"),
        check_vma=False,
    )
```

```python
import functools

import jax
import jax.numpy as jnp
from jax import lax
from jax.experimental import pallas as pl
from jax.experimental.pallas import tpu as pltpu
from jax.sharding import PartitionSpec as P

KB = 32
RB = 2
CB = 16
STEPS = 2
FIRST = 6
KEEP = 8
MORE = 4
GRANT = 56 << 20
NOTE = 8

VMEM = pl.BlockSpec(memory_space=pltpu.VMEM)
SMEM = pl.BlockSpec(memory_space=pltpu.SMEM)
ANY = pl.BlockSpec(memory_space=pl.ANY)


def cost(flops, size):
    return pl.CostEstimate(flops=flops, bytes_accessed=4 * size, transcendentals=0)


def pack_kernel(count, pieces, pos_ref, a_ref, out_ref, sem):
    stored, edge = a_ref.shape[0], a_ref.shape[1]
    span = count * edge + NOTE
    lane = lax.broadcasted_iota(jnp.int32, (NOTE, edge), 1)
    line = lax.broadcasted_iota(jnp.int32, (NOTE, edge), 0)
    notes = [jnp.zeros((NOTE, edge), jnp.int32) for _ in range(pieces)]
    places = [jnp.int32(0) for _ in range(pieces)]
    for m in range(stored):
        row, col = pos_ref[0, m], pos_ref[1, m]
        piece = col // KB
        at = places[-1]
        for h in range(pieces - 1):
            at = jnp.where(piece == h, places[h], at)
        start = pl.multiple_of(piece * span + at * edge, 8)
        pltpu.make_async_copy(a_ref.at[m], out_ref.at[pl.ds(start, edge)], sem).start()
        for h in range(pieces):
            mine = piece == h
            hit = mine & (lane == at)
            notes[h] = jnp.where(hit & (line == 0), row, notes[h])
            notes[h] = jnp.where(hit & (line == 1), col % KB, notes[h])
            places[h] = places[h] + mine.astype(jnp.int32)
    for h in range(pieces):
        out_ref[pl.ds(h * span + count * edge, NOTE), :] = notes[h].astype(jnp.float32)
    for m in range(stored):
        pltpu.make_async_copy(a_ref.at[m], out_ref.at[pl.ds(m * edge, edge)], sem).wait()


def pack(pos, blocks, count):
    stored, edge = blocks.shape[:2]
    pieces = stored // count
    return pl.pallas_call(
        functools.partial(pack_kernel, count, pieces),
        out_shape=jax.ShapeDtypeStruct((pieces * (count * edge + NOTE), edge), jnp.float32),
        in_specs=[SMEM, ANY],
        out_specs=VMEM,
        scratch_shapes=[pltpu.SemaphoreType.DMA],
        compiler_params=pltpu.CompilerParams(vmem_limit_bytes=8 << 20),
        cost_estimate=cost(0, 2 * blocks.size),
    )(pos, blocks)


def select_kernel(half_ref, here_ref, there_ref, b_pos_ref, b_ref, keep_ref, more_ref, rest_ref, got, lut, index, sems):
    for k in range(KB):
        lut[k] = 0
    for m in range(here_ref.shape[1]):
        column = here_ref[1, m] + there_ref[1, m]

        @pl.when(column // KB == half_ref[0])
        def _():
            lut[column % KB] = 1

    n = jnp.int32(0)
    for m in range(FIRST, b_ref.shape[0]):
        index[n] = m
        n = n + lut[b_pos_ref[0, m]]

    def fetch(k):
        return pltpu.make_async_copy(b_ref.at[index[k]], got.at[k], sems.at[0])

    pl.loop(0, n)(lambda k: fetch(k).start())
    pl.loop(0, n)(lambda k: fetch(k).wait())
    for act in ("start", "wait"):
        for out, start, on in (
            (keep_ref, 0, n > 0),
            (more_ref, KEEP, (n > KEEP) & (n <= KEEP + MORE)),
            (rest_ref, KEEP, n > KEEP + MORE),
        ):

            @pl.when(on)
            def _():
                getattr(pltpu.make_async_copy(got.at[pl.ds(start, out.shape[0])], out, sems.at[1]), act)()


def select(half, asked, b_pos, b):
    tile = b.shape[0]
    sizes = (KEEP, MORE, tile - FIRST - KEEP)
    return pl.pallas_call(
        select_kernel,
        out_shape=tuple(jax.ShapeDtypeStruct((n,) + b.shape[1:], b.dtype) for n in sizes),
        in_specs=[SMEM] * 4 + [ANY],
        out_specs=(ANY,) * len(sizes),
        scratch_shapes=[
            pltpu.VMEM((tile - FIRST,) + b.shape[1:], b.dtype),
            pltpu.SMEM((KB,), jnp.int32),
            pltpu.SMEM((tile + 1,), jnp.int32),
            pltpu.SemaphoreType.DMA((2,)),
        ],
        compiler_params=pltpu.CompilerParams(vmem_limit_bytes=GRANT),
        cost_estimate=cost(0, b.size),
    )(half, *asked, b_pos, b)


def split(x):
    high = x.astype(jnp.bfloat16)
    return high, (x - high.astype(jnp.float32)).astype(jnp.bfloat16)


def product(a_wide, b):
    high, low = split(b)
    wide = jnp.concatenate(
        [jnp.concatenate([high, low], axis=1), jnp.concatenate([high, jnp.zeros_like(low)], axis=1)], axis=0
    )
    both = jnp.dot(a_wide, wide, preferred_element_type=jnp.float32)
    edge = b.shape[1]
    return both[:, :edge] + both[:, edge:]


def listed(lut, lists, a_pos_ref, b_pos_ref, first, stop):
    for k in range(KB):
        lut[k] = -1
    for m in range(a_pos_ref.shape[1]):
        lut[a_pos_ref[1, m]] = m
    n = jnp.int32(0)
    for m in range(first, stop):
        which = lut[b_pos_ref[0, m]]
        lists[0, n] = which
        lists[1, n] = a_pos_ref[0, jnp.maximum(which, 0)]
        lists[2, n] = b_pos_ref[1, m]
        lists[3, n] = m
        n = n + (which >= 0).astype(jnp.int32)
    return n


def add_listed(lists, low, high, a_wide, b_block, out_ref, after=None):
    edge = a_wide.shape[1]

    def one(n):
        return product(a_wide[lists[0, n]], b_block(n))

    def put(n, part):
        row = pl.multiple_of(lists[1, n] * edge, edge)
        col = pl.multiple_of(lists[2, n] * edge, edge)
        out_ref[pl.ds(row, edge), pl.ds(col, edge)] += part
        if after is not None:
            after(n)

    pairs = jnp.maximum(high - low, 0) // 2

    @pl.loop(0, pairs)
    def _(t):
        n = low + 2 * t
        parts = one(n), one(n + 1)
        put(n, parts[0])
        put(n + 1, parts[1])

    @pl.when(low + 2 * pairs < high)
    def _():
        put(high - 1, one(high - 1))


def widen(a_wide, x):
    count, edge = a_wide.shape[:2]
    for m in range(count):
        high, low = split(x[pl.ds(m * edge, edge), :])
        a_wide[m, :, :edge] = high
        a_wide[m, :, edge:] = low


def spot(ref, edge, row, col):
    rows = pl.ds(pl.multiple_of(row * edge, edge), edge)
    return ref.at[rows, pl.ds(pl.multiple_of(col * edge, edge), edge)]


def level(n):
    return (n > KEEP).astype(jnp.int32) + (n > KEEP + MORE).astype(jnp.int32)


def early_kernel(rows, cols, *refs):
    (first_ref, next_pos_ref, here_ref, there_ref, pos0_ref, pos1_ref, b_pos_ref), refs = refs[:7], refs[7:]
    my_row, my_col = lax.axis_index("row"), lax.axis_index("col")
    tiles = [lax.rem(my_row + s, rows) for s in range(STEPS)]
    halves = [lax.rem(tile, rows // cols) for tile in tiles]
    near = [lax.rem(my_col, 2) == lax.rem(tile // (rows // cols), 2) for tile in tiles]
    mine_ref, other_ref, b_ref, out_ref, wide_out, plan, code_ref, *refs = refs
    acc, nought, x0, x1, b_v, first_v, wide0, wide1, lut, lists, firsts, seen, sems = refs
    sem, wide_copy = sems.at[0], pltpu.make_async_copy(wide1, wide_out, sems.at[1])
    count, edge = wide0.shape[:2]
    tile = b_pos_ref.shape[1]
    span = count * edge + NOTE

    def load(s, src, x):
        start = pl.multiple_of(halves[s] * span, 8)
        return pltpu.make_async_copy(src.at[pl.ds(start, count * edge)], x, sems.at[2 + s])

    for s, x in enumerate((x0, x1)):
        for src, on in ((mine_ref, near[s]), (other_ref, jnp.logical_not(near[s]))):

            @pl.when(on)
            def _():
                load(s, src, x).start()

    def block(k):
        return pltpu.make_async_copy(b_ref.at[lists[3, k]], b_v.at[k], sems.at[4])

    def early_block(k):
        start = pl.multiple_of(firsts[3, k] * edge, edge)
        return pltpu.make_async_copy(first_ref.at[pl.ds(start, edge)], first_v.at[k], sems.at[5])

    n = listed(lut, lists, pos0_ref, b_pos_ref, 0, tile)
    pl.loop(0, n)(lambda k: block(k).start())
    n1 = listed(lut, firsts, pos1_ref, next_pos_ref, 0, FIRST)
    pl.loop(0, n1)(lambda k: early_block(k).start())
    for k in range(RB * CB):
        seen[k] = 0
    nought[...] = jnp.zeros_like(nought)

    def touch(list_ref):
        def act(k):
            row, col = list_ref[1, k], list_ref[2, k]
            seen[row * CB + col] = 1
            spot(acc, edge, row, col)[...] = nought[...]

        return act

    pl.loop(0, n)(touch(lists))
    pl.loop(0, n1)(touch(firsts))
    for row in range(RB):
        for col in range(CB):

            @pl.when(seen[row * CB + col] == 0)
            def _():
                pltpu.make_async_copy(nought, spot(out_ref, edge, row, col), sem).start()

    load(1, mine_ref, x1).wait()
    widen(wide1, x1)
    wide_copy.start()
    load(0, mine_ref, x0).wait()
    widen(wide0, x0)
    pl.loop(0, n)(lambda k: block(k).wait())
    add_listed(lists, 0, n, wide0, lambda k: b_v[k], acc)
    pl.loop(0, n1)(lambda k: early_block(k).wait())
    add_listed(firsts, 0, n1, wide1, lambda k: first_v[k], acc)
    for row in range(RB):
        for col in range(CB):

            @pl.when(seen[row * CB + col] == 1)
            def _():
                pltpu.make_async_copy(spot(acc, edge, row, col), spot(out_ref, edge, row, col), sem).start()

    gets = listed(lut, plan, pos1_ref, next_pos_ref, FIRST, tile)
    plan[0, tile] = gets
    for k in range(KB):
        lut[k] = 0
    for m in range(here_ref.shape[1]):
        column = here_ref[1, m] + there_ref[1, m]

        @pl.when(column // KB == halves[0])
        def _():
            lut[column % KB] = 1

    gives = jnp.int32(0)
    for m in range(FIRST, tile):
        gives = gives + lut[b_pos_ref[0, m]]
    even = lax.rem(my_row, 2) == 0
    code_ref[0] = level(jnp.where(even, gets, gives)) + 4 * level(jnp.where(even, gives, gets))
    pltpu.make_async_copy(acc, out_ref, sem).wait()
    wide_copy.wait()


def early(rows, cols, first_b, coords, mine, other, b):
    tile, edge = b.shape[:2]
    count = coords[3].shape[1]
    wide = (count, edge, 2 * edge)
    total = (RB * edge, CB * edge)
    return pl.pallas_call(
        functools.partial(early_kernel, rows, cols),
        out_shape=(
            jax.ShapeDtypeStruct(total, jnp.float32),
            jax.ShapeDtypeStruct(wide, jnp.bfloat16),
            jax.ShapeDtypeStruct((4, tile + 1), jnp.int32),
            jax.ShapeDtypeStruct((1,), jnp.int32),
        ),
        in_specs=[ANY] + [SMEM] * len(coords) + [ANY] * 3,
        out_specs=(ANY, ANY, SMEM, SMEM),
        scratch_shapes=[
            pltpu.VMEM(total, jnp.float32),
            pltpu.VMEM((edge, edge), jnp.float32),
            pltpu.VMEM((count * edge, edge), jnp.float32),
            pltpu.VMEM((count * edge, edge), jnp.float32),
            pltpu.VMEM(b.shape, jnp.float32),
            pltpu.VMEM((FIRST, edge, edge), jnp.float32),
            pltpu.VMEM(wide, jnp.bfloat16),
            pltpu.VMEM(wide, jnp.bfloat16),
            pltpu.SMEM((KB,), jnp.int32),
            pltpu.SMEM((4, tile + 1), jnp.int32),
            pltpu.SMEM((4, tile + 1), jnp.int32),
            pltpu.SMEM((RB * CB,), jnp.int32),
            pltpu.SemaphoreType.DMA((6,)),
        ],
        compiler_params=pltpu.CompilerParams(vmem_limit_bytes=48 << 20),
        cost_estimate=cost(6 * b.size * edge, 2 * b.size),
    )(first_b, *coords, mine, other, b)


def empty(shapes):
    return pl.pallas_call(
        lambda *refs: None,
        out_shape=tuple(jax.ShapeDtypeStruct(x, jnp.float32) for x in shapes),
        out_specs=(ANY,) * len(shapes),
    )()


def late_kernel(side_ref, plan, wide_ref, kept_ref, total_ref, *refs):
    sides, (out_ref, acc, wide, got, seen, sems) = refs[:4], refs[4:]
    edge = wide.shape[1]
    tile = plan.shape[1] - 1
    n = plan[0, tile]

    def load(row, col):
        return pltpu.make_async_copy(spot(out_ref, edge, row, col), spot(acc, edge, row, col), sems.at[2])

    def store(row, col):
        return pltpu.make_async_copy(spot(acc, edge, row, col), spot(out_ref, edge, row, col), sems.at[3])

    def touched(act):
        for row in range(RB):
            for col in range(CB):

                @pl.when(seen[row * CB + col] > 0)
                def _():
                    act(row, col)

    @pl.when(n > 0)
    def _():
        def fetch(act):
            getattr(pltpu.make_async_copy(wide_ref, wide, sems.at[4]), act)()
            getattr(pltpu.make_async_copy(kept_ref, got.at[pl.ds(0, KEEP)], sems.at[0]), act)()

        def fetch_more(act):
            for side in range(2):
                more, rest = sides[2 * side : 2 * side + 2]
                for src, on in ((more, (n > KEEP) & (n <= KEEP + MORE)), (rest, n > KEEP + MORE)):

                    @pl.when((side_ref[0] == side) & on)
                    def _():
                        getattr(pltpu.make_async_copy(src, got.at[pl.ds(KEEP, src.shape[0])], sems.at[1]), act)()

        fetch("start")
        for k in range(RB * CB):
            seen[k] = 0

        @pl.loop(0, n)
        def _(k):
            row, col = plan[1, k], plan[2, k]

            @pl.when(seen[row * CB + col] == 0)
            def _():
                load(row, col).start()

            seen[row * CB + col] = k + 1

        fetch_more("start")
        fetch("wait")
        touched(lambda row, col: load(row, col).wait())

        def after(k):
            row, col = plan[1, k], plan[2, k]

            @pl.when(seen[row * CB + col] == k + 1)
            def _():
                store(row, col).start()

        add_listed(plan, 0, jnp.minimum(n, KEEP), wide, lambda k: got[k], acc, after)
        fetch_more("wait")
        add_listed(plan, jnp.minimum(n, KEEP), n, wide, lambda k: got[k], acc, after)
        touched(lambda row, col: store(row, col).wait())


def late(side, plan, wide, kept_b, total, sides):
    edge = kept_b.shape[1]
    tile = plan.shape[1] - 1
    return pl.pallas_call(
        late_kernel,
        out_shape=jax.ShapeDtypeStruct(total.shape, total.dtype),
        in_specs=[SMEM] * 2 + [ANY] * 7,
        out_specs=ANY,
        input_output_aliases={4: 0},
        scratch_shapes=[
            pltpu.VMEM(total.shape, jnp.float32),
            pltpu.VMEM(wide.shape, wide.dtype),
            pltpu.VMEM((tile - FIRST, edge, edge), jnp.float32),
            pltpu.SMEM((RB * CB,), jnp.int32),
            pltpu.SemaphoreType.DMA((5,)),
        ],
        compiler_params=pltpu.CompilerParams(vmem_limit_bytes=12 << 20),
        cost_estimate=cost(6 * tile * edge**3, 2 * total.size),
    )(side, plan, wide, kept_b, total, *sides)


def per_device(a_blocks, a_coords, b_blocks, b_coords):
    rows, cols = lax.axis_size("row"), lax.axis_size("col")
    per_col = rows // cols
    my_row, my_col = lax.axis_index("row"), lax.axis_index("col")
    a, a_pos, b, b_pos = a_blocks[0, 0], a_coords[0, 0], b_blocks[0, 0], b_coords[0, 0]
    count = a.shape[0] // per_col
    edge, tile = a.shape[1], b.shape[0]

    def send(x, pairs):
        flat = [(r * cols + c, s * cols + d) for (r, c), (s, d) in pairs]
        return lax.ppermute(x, ("row", "col"), flat)

    def ring(x):
        return lax.ppermute(x, "row", [((r + 1) % rows, r) for r in range(rows)])

    def owner(row, step):
        return (row + step) % rows // per_col

    everywhere = [(r, c) for r in range(rows) for c in range(cols)]
    swap = [((r, c), (r, c ^ 1)) for r, c in everywhere]

    note = jnp.pad(b_pos.astype(jnp.float32), ((0, NOTE - 2), (0, edge - tile)))
    first_b = jnp.concatenate([b[:FIRST].reshape(FIRST * edge, edge), note])
    first_b, a_pos = lax.optimization_barrier((first_b, a_pos))
    first_b = ring(first_b)
    next_pos = first_b[FIRST * edge : FIRST * edge + 2, :tile].astype(jnp.int32)
    asked = 0
    for d in range(0, cols, 2):
        pairs = [((r, owner(r, 1)), ((r + 1) % rows, (owner(r, 1) + d) % cols)) for r in range(rows)]
        asked = asked + send(a_pos, pairs)
    packed = pack(a_pos, a, count)
    got = 0
    for d in range(2, cols, 2):
        pairs = sorted({((r, owner(r, s)), (r, (owner(r, s) + d) % cols)) for r in range(rows) for s in range(STEPS)})
        got = got + send(packed, pairs)
    owners = [owner(my_row, s) for s in range(STEPS)]
    own = functools.reduce(jnp.logical_or, [my_col == o for o in owners])

    asked = asked, send(asked, swap)
    half = (my_row % per_col).astype(jnp.int32)
    keep_b, more_b, rest_b = select(half[None], asked, b_pos, b)
    kept_b = ring(keep_b)

    got, _ = lax.optimization_barrier((got, keep_b))
    mine = jnp.where(own, packed, got)
    other = send(mine, swap)

    def notes_of(x):
        return x.reshape(per_col, -1, edge)[:, count * edge : count * edge + 2, :count].astype(jnp.int32)

    pos = []
    mine_notes, other_notes = notes_of(mine), notes_of(other)
    for s in range(STEPS):
        h, near = (my_row + s) % per_col, my_col % 2 == owners[s] % 2
        pos.append(lax.dynamic_index_in_dim(jnp.where(near, mine_notes, other_notes), h, keepdims=False))

    total, wide, plan, code = early(rows, cols, first_b, (next_pos, *asked, *pos, b_pos), mine, other, b)

    sides, code = [], jnp.maximum(code[0], 0)
    for parity in range(2):
        pairs = [(((r + 1) % rows, c), (r, c)) for r in range(parity, rows, 2) for c in range(cols)]

        def none():
            return empty((more_b.shape, rest_b.shape))

        def small():
            return send(more_b, pairs), *empty((rest_b.shape,))

        def full():
            return *empty((more_b.shape,)), send(rest_b, pairs)

        which = jnp.bitwise_and(lax.shift_right_logical(code, 2 * parity), 3)
        sides += lax.switch(which, [none, small, full])

    side = (my_row % 2).astype(jnp.int32)[None]
    return late(side, plan, wide, kept_b, total, sides)


def solution(mesh):
    return jax.shard_map(
        per_device,
        mesh=mesh,
        in_specs=(
            P("row", "col", None, None, None),
            P("row", "col", None, None),
            P("row", "col", None, None, None),
            P("row", "col", None, None),
        ),
        out_specs=P("row", "col"),
        check_vma=False,
    )
```
